32 devices in a mesh: groups: 2 (over y), sig: 4 (over z), build: 4 (over x, core).
Axes of the slice: x: 2, y: 2, z: 4, core: 2. Of those that a mesh axis runs over, the one named last changes fastest.
Arguments:
- tiles: bfloat16 [8, 4, 32, 256, 256], P(('groups', 'sig'), 'build'), parts along dimension 0, may hold values from 0 to 15, as said below
- tile_rows: int32 [8, 4, 32], P(('groups', 'sig'), 'build'), parts along dimension 0, may hold values from 0 to 7, as said below
- tile_cols: int32 [8, 4, 32], P(('groups', 'sig'), 'build'), parts along dimension 0, may hold values from 0 to 7
- tile_count: int32 [8, 4], P(('groups', 'sig'), 'build'), parts along dimension 0, may hold values from 1 to 32, as said below
- factor_w: bfloat16 [16384, 128], P(('groups', 'sig', 'build')), parts along dimension 0, as said below
- factor_h: bfloat16 [16384, 128], P(('groups', 'sig', 'build')), parts along dimension 0, as said below
- tv_weight: float32 [256], P('groups'), parts along dimension 0, may hold values from 0.05 to 0.6
Outputs:
- w_new: bfloat16 [16384, 128], P(('groups', 'sig', 'build')), parts along dimension 0
- smooth: float32 [16384, 128], P(('groups', 'sig', 'build')), parts along dimension 0
The draws below stay inside these ranges and needn't reach their ends.
There are 2 independent parts, one for each index of `groups`. The reference program is written for one: setup_inputs(seed, part) draws one part's arguments, and reference() takes and returns one part's arrays. A program takes and returns all parts, laid end to end along the dimension named above; each array names one. Nothing has to cross between parts.
Inputs may be any that keep to these rules, and one draw needn't show every extreme that they name: `tiles`: nonnegative integer counts. Within one block all slots name distinct (tile_rows, tile_cols) pairs. Slots from tile_count on hold no data; some block uses all 32 slots. `factor_w`: positive entries. `factor_h`: positive entries.
All inputs are finite; a program needn't handle non-finite values.
Results may differ from the reference program's by a relative error of at most 0.0045.
Values may be sent and summed in bfloat16 or wider, within the bound.
A program may use at most 64 MiB of HBM per device.

```python
import math
import jax
import jax.numpy as jnp
from jax import lax

RANK = 128
TILE = 256
ROWS_DEV = 2048
COLS_DEV = 2048
TILES_DEV = 32
TV_STEPS = 16
SIGS = 8192
BUILDS = 8192
N_SIG = 4
N_BUILD = 4


DAMPING = 0.0078125


def block_order(key):
    base = jax.random.fold_in(key, 17)
    blocks = N_SIG * N_BUILD
    places = ROWS_DEV // TILE * (COLS_DEV // TILE)
    keys = jax.random.split(base, blocks)
    orders = jax.vmap(lambda single: jax.random.permutation(single, places))(keys)
    return orders[:, :TILES_DEV].reshape(N_SIG, N_BUILD, TILES_DEV).astype(jnp.int32)


def row_component(key):
    base = jax.random.fold_in(key, 31)
    return jax.random.randint(base, (ROWS_DEV * N_SIG,), 0, RANK).astype(jnp.int32)


def draw_tile_rows(key, part):
    return (block_order(key) // (COLS_DEV // TILE)).astype(jnp.int32)


def draw_tile_cols(key, part):
    return (block_order(key) % (COLS_DEV // TILE)).astype(jnp.int32)


def draw_tile_count(key, part):
    blocks = N_SIG * N_BUILD
    first = jax.random.randint(jax.random.fold_in(key, 1), (blocks,), 1, TILES_DEV + 1)
    second = jax.random.randint(jax.random.fold_in(key, 2), (blocks,), 1, TILES_DEV + 1)
    fullest = jax.random.randint(jax.random.fold_in(key, 3), (), 0, blocks)
    counts = jnp.where(jnp.arange(blocks) == fullest, TILES_DEV, jnp.minimum(first, second))
    return counts.reshape(N_SIG, N_BUILD).astype(jnp.int32)


def draw_tiles(key, part):
    order = block_order(key)
    component = row_component(key)
    key = jax.random.fold_in(key, 5)
    col_tiles = COLS_DEV // TILE
    shard_width = COLS_DEV // N_SIG
    offsets = jnp.arange(TILE, dtype=jnp.int32)
    sig_ids = jnp.arange(N_SIG, dtype=jnp.int32)[:, None, None, None]
    build_ids = jnp.arange(N_BUILD, dtype=jnp.int32)[None, :, None, None]
    global_rows = sig_ids * ROWS_DEV + (order // col_tiles)[..., None] * TILE + offsets
    local_cols = (order % col_tiles)[..., None] * TILE + offsets
    global_cols = (local_cols // shard_width * N_BUILD + build_ids) * shard_width + local_cols % shard_width
    exponents = jax.random.randint(jax.random.fold_in(key, 7), (RANK, COLS_DEV * N_BUILD), 1, 5)
    levels = (2 ** exponents - 1).astype(jnp.int32)
    row_comp = jnp.take(component, global_rows, axis=0)
    tops = levels[row_comp[..., :, None], global_cols[..., None, :]]
    shape = (N_SIG, N_BUILD, TILES_DEV, TILE, TILE)
    counts = jax.random.randint(jax.random.fold_in(key, 9), shape, 0, tops + 1)
    return counts.astype(jnp.float32).astype(jnp.bfloat16)


def rising(length):
    position = jnp.arange(length, dtype=jnp.float32) / length
    return jnp.exp(jnp.log(10.0) * (position - 0.5))


def draw_factor_w(key, part):
    component = row_component(key)
    key = jax.random.fold_in(key, 21)
    length = ROWS_DEV * N_SIG
    spread = jnp.exp(jax.random.uniform(key, (length, RANK), jnp.float32, -1.0, 1.0))
    leading = component[:, None] == jnp.arange(RANK, dtype=jnp.int32)[None, :]
    damp = jnp.where(leading, 1.0, DAMPING)
    return (0.5 * rising(length)[:, None] * spread * damp).astype(jnp.bfloat16)


def draw_factor_h(key, part):
    key = jax.random.fold_in(key, 23)
    length = COLS_DEV * N_BUILD
    spread = jnp.exp(jax.random.uniform(key, (length, RANK), jnp.float32, -1.0, 1.0))
    return (0.5 * rising(length)[:, None] * spread).astype(jnp.bfloat16)


def setup_inputs(seed: int = 0, part: int = 0) -> dict:
    streams_of = jax.random.split(jax.random.key(seed), 8)
    part_splits = jax.random.split(jax.random.fold_in(streams_of[7], part), 8)
    tiles = draw_tiles(jax.random.fold_in(jax.random.fold_in(streams_of[7], part), 71), part)
    tile_rows = draw_tile_rows(jax.random.fold_in(jax.random.fold_in(streams_of[7], part), 71), part)
    tile_cols = draw_tile_cols(jax.random.fold_in(jax.random.fold_in(streams_of[7], part), 71), part)
    tile_count = draw_tile_count(jax.random.fold_in(jax.random.fold_in(streams_of[7], part), 71), part)
    factor_w = draw_factor_w(jax.random.fold_in(jax.random.fold_in(streams_of[7], part), 71), part)
    factor_h = draw_factor_h(jax.random.fold_in(jax.random.fold_in(streams_of[7], part), 71), part)
    tv_weight = jnp.clip(jnp.exp(jax.random.uniform(part_splits[6], (RANK,), jnp.float32, math.log(0.05), math.log(0.6))), 0.05, 0.6)
    return dict(tiles=tiles, tile_rows=tile_rows, tile_cols=tile_cols, tile_count=tile_count, factor_w=factor_w, factor_h=factor_h, tv_weight=tv_weight)


TAU = 0.25


def reference(tiles, tile_rows, tile_cols, tile_count, factor_w, factor_h, tv_weight):
    row_tiles = ROWS_DEV // TILE
    col_tiles = COLS_DEV // TILE
    shard_width = COLS_DEV // N_SIG
    blocks = N_SIG * N_BUILD
    flat_tiles = tiles.reshape(blocks, TILES_DEV, TILE, TILE)
    flat_rows = tile_rows.reshape(blocks, TILES_DEV)
    flat_cols = tile_cols.reshape(blocks, TILES_DEV)
    flat_count = tile_count.reshape(blocks)
    slot_ids = jnp.arange(TILES_DEV, dtype=jnp.int32)
    block_ids = jnp.arange(blocks, dtype=jnp.int32)

    def chosen_pair(block_id, h_now):
        sig_id = (block_id // N_BUILD).astype(jnp.int32)
        build_id = (block_id % N_BUILD).astype(jnp.int32)
        w_rows = lax.dynamic_slice_in_dim(factor_w, sig_id * ROWS_DEV, ROWS_DEV, 0).reshape(row_tiles, TILE, RANK)
        h_grid = h_now.reshape(N_SIG, N_BUILD, shard_width, RANK)
        h_cols = lax.dynamic_slice_in_dim(h_grid, build_id, 1, 1).reshape(col_tiles, TILE, RANK)
        w_chosen = jnp.take(w_rows, flat_rows[block_id], axis=0).astype(jnp.float32)
        h_chosen = jnp.take(h_cols, flat_cols[block_id], axis=0).astype(jnp.float32)
        product = jnp.einsum("sik,sjk->sij", w_chosen, h_chosen)
        live_mask = (slot_ids < flat_count[block_id])[:, None, None]
        ratio_tile = jnp.where(live_mask, flat_tiles[block_id].astype(jnp.float32) / product, 0.0).astype(jnp.bfloat16)
        ratio_tile = lax.optimization_barrier(ratio_tile).astype(jnp.float32)
        return sig_id, build_id, w_chosen, h_chosen, ratio_tile

    def column_pass(numer_grid, block_id):
        sig_id, build_id, w_chosen, h_chosen, ratio_tile = chosen_pair(block_id, factor_h)
        contrib = jnp.einsum("sij,sik->sjk", ratio_tile, w_chosen)
        onehot = (flat_cols[block_id][:, None] == jnp.arange(col_tiles, dtype=jnp.int32)[None, :]).astype(jnp.float32)
        summed = jnp.einsum("sc,sjk->cjk", onehot, contrib, precision=lax.Precision.HIGHEST)
        summed = summed.reshape(N_SIG, 1, shard_width, RANK)
        current = lax.dynamic_slice_in_dim(numer_grid, build_id, 1, 1)
        return lax.dynamic_update_slice_in_dim(numer_grid, current + summed, build_id, 1), None

    numer_grid, _ = lax.scan(column_pass, jnp.zeros((N_SIG, N_BUILD, shard_width, RANK), jnp.float32), block_ids)
    numer_h = numer_grid.reshape(BUILDS, RANK)
    col_total = jnp.sum(factor_w.astype(jnp.float32), axis=0)
    h_new = (factor_h.astype(jnp.float32) * numer_h / col_total).astype(jnp.bfloat16)

    def row_pass(numer_w, block_id):
        sig_id, build_id, w_chosen, h_chosen, ratio_tile = chosen_pair(block_id, h_new)
        contrib = jnp.einsum("sij,sjk->sik", ratio_tile, h_chosen)
        onehot = (flat_rows[block_id][:, None] == jnp.arange(row_tiles, dtype=jnp.int32)[None, :]).astype(jnp.float32)
        summed = jnp.einsum("sr,sik->rik", onehot, contrib, precision=lax.Precision.HIGHEST).reshape(ROWS_DEV, RANK)
        current = lax.dynamic_slice_in_dim(numer_w, sig_id * ROWS_DEV, ROWS_DEV, 0)
        return lax.dynamic_update_slice_in_dim(numer_w, current + summed, sig_id * ROWS_DEV, 0), None

    numer_w, _ = lax.scan(row_pass, jnp.zeros((SIGS, RANK), jnp.float32), block_ids)
    row_total = jnp.sum(h_new.astype(jnp.float32), axis=0)
    w_new = (factor_w.astype(jnp.float32) * numer_w / row_total).astype(jnp.bfloat16)

    signal = h_new.astype(jnp.float32)
    dual_state = jnp.zeros((BUILDS, RANK), jnp.float32)
    last_mask = (jnp.arange(BUILDS, dtype=jnp.int32) < BUILDS - 1).astype(jnp.float32)[:, None]
    zero_row = jnp.zeros((1, RANK), jnp.float32)
    for repeat in range(TV_STEPS):
        before = jnp.concatenate([zero_row, dual_state[:-1]], axis=0)
        primal = signal - before + dual_state
        after = jnp.concatenate([primal[1:], zero_row], axis=0)
        dual_state = jnp.clip(dual_state + TAU * (after - primal), -tv_weight, tv_weight) * last_mask
    before = jnp.concatenate([zero_row, dual_state[:-1]], axis=0)
    smooth = signal - before + dual_state
    return w_new, smooth
```

```python
import functools

import jax
import jax.numpy as jnp
from jax import lax
from jax.experimental import pallas as pl
from jax.experimental.pallas import tpu as pltpu
from jax.sharding import PartitionSpec as P

TV_STEPS = 16
TAU = 0.25
HALO = 32
GROUP = 4
MESH = pl.DeviceIdType.MESH


def kernel(
    n_sig, n_build,
    meta, tiles_hbm, fw_ref, fh_ref, tv_ref,
    w_out, smooth_out,
    tiles, w_blk, w_turn, h_blk, h_next, w_tiles, h_tiles, chain_h, chain_w, numer,
    h_send, h_recv, w_send, w_recv, col_part, row_part, ext,
    tile_sem, send_w, recv_w, send_h, recv_h, send_ct, recv_ct, send_nh, recv_nh,
    send_h2, recv_h2, send_halo, recv_halo, send_rt, recv_rt, send_nw, recv_nw,
):
    f32, bf16 = jnp.float32, jnp.bfloat16
    sig = lax.axis_index("sig")
    build = lax.axis_index("build")
    slots, tile = tiles.shape[0], tiles.shape[1]
    w_rows, h_rows = fw_ref.shape[0], fh_ref.shape[0]
    row_tiles = w_blk.shape[0] // tile
    col_tiles = h_blk.shape[0] // tile

    load = pltpu.make_async_copy(tiles_hbm, tiles, tile_sem)
    load.start()

    def sig_peer(k):
        return lax.rem(sig + k, n_sig)

    def build_peer(k):
        return lax.rem(build + k, n_build)

    total = n_sig * n_build
    index = sig * n_build + build
    above = lax.rem(index + 1, total)
    below = lax.rem(index + total - 1, total)

    def at(linear):
        return {"sig": lax.div(linear, n_build), "build": lax.rem(linear, n_build)}

    barrier = pltpu.get_barrier_semaphore()
    for k in range(1, n_sig):
        pl.semaphore_signal(barrier, inc=1, device_id={"sig": sig_peer(k)}, device_id_type=MESH)
    for k in range(1, n_build):
        pl.semaphore_signal(barrier, inc=1, device_id={"build": build_peer(k)}, device_id_type=MESH)
    pl.semaphore_signal(barrier, inc=1, device_id=at(above), device_id_type=MESH)
    pl.semaphore_signal(barrier, inc=1, device_id=at(below), device_id_type=MESH)
    pl.semaphore_wait(barrier, n_sig + n_build)

    def remote(src, dst, send, recv, device):
        copy = pltpu.make_async_remote_copy(
            src_ref=src, dst_ref=dst, send_sem=send, recv_sem=recv,
            device_id=device, device_id_type=MESH,
        )
        copy.start()
        return copy

    def rows_of(place, rows):
        return pl.ds(pl.multiple_of(place * rows, rows), rows)

    pending = []

    h_copies = [
        remote(fh_ref, h_blk.at[rows_of(sig, h_rows)], send_h.at[k], recv_h.at[k], {"sig": sig_peer(k)})
        for k in range(1, n_sig)
    ]
    w_copies = [
        remote(fw_ref, w_blk.at[rows_of(build, w_rows)], send_w.at[k], recv_w.at[k], {"build": build_peer(k)})
        for k in range(1, n_build)
    ]
    pending += h_copies + w_copies
    h_blk[rows_of(sig, h_rows), :] = fh_ref[...]
    w_blk[rows_of(build, w_rows), :] = fw_ref[...]
    chain_h[0] = jnp.zeros(chain_h.shape[1:], f32)
    chain_w[0] = jnp.zeros(chain_w.shape[1:], f32)

    for copy in w_copies:
        copy.wait_recv()
    part = jnp.zeros((8, w_blk.shape[1]), f32)
    for r in range(row_tiles):
        block = w_blk[r * tile:(r + 1) * tile, :]
        w_tiles[r] = block
        w_turn[r] = block.T
        part += block.astype(f32).reshape(tile // 8, 8, -1).sum(axis=0)
    col_part[sig] = part
    ct_copies = [
        remote(col_part.at[sig], col_part.at[sig], send_ct.at[k], recv_ct.at[k], {"sig": sig_peer(k)})
        for k in range(1, n_sig)
    ]
    pending += ct_copies

    load.wait()
    for copy in h_copies:
        copy.wait_recv()
    for c in range(col_tiles):
        h_tiles[0, c] = h_blk[c * tile:(c + 1) * tile, :]

    def ratio_of(slot, w, h):
        product = lax.dot_general(w, h, (((1,), (1,)), ((), ())), preferred_element_type=f32)
        return (tiles[slot].astype(f32) / product).astype(bf16)

    def pass_h(step, carry):
        terms = []
        for g in range(GROUP):
            slot = step * GROUP + g
            row, col = meta[0, slot], meta[1, slot]
            ratio = ratio_of(slot, w_tiles[row], h_tiles[0, col])
            terms.append(jnp.dot(w_turn[row], ratio, preferred_element_type=f32))
        for g in range(GROUP):
            slot = step * GROUP + g
            chain_h[slot + 1] = chain_h[meta[1, slots + slot]] + terms[g]
        return carry

    lax.fori_loop(0, slots // GROUP, pass_h, 0)
    for c in range(col_tiles):
        block = chain_h[meta[1, 2 * slots + c]].T
        numer[c * tile:(c + 1) * tile, :] = block
        h_send[c * tile:(c + 1) * tile, :] = block.astype(bf16)
    nh_copies = [
        remote(h_send.at[rows_of(sig_peer(k), h_rows)], h_recv.at[sig], send_nh.at[k], recv_nh.at[k],
               {"sig": sig_peer(k)})
        for k in range(1, n_sig)
    ]
    pending += nh_copies
    for copy in ct_copies:
        copy.wait_recv()
    col_sum = col_part[0]
    for k in range(1, n_sig):
        col_sum += col_part[k]
    col_total = jnp.sum(col_sum, axis=0, keepdims=True)
    share = numer[rows_of(sig, h_rows), :]
    for k in range(1, n_sig):
        nh_copies[k - 1].wait_recv()
        share += h_recv[sig_peer(n_sig - k)].astype(f32)
    h_new = (fh_ref[...].astype(f32) * share / col_total).astype(bf16)
    mine = rows_of(sig, h_rows)
    h_next[mine, :] = h_new
    ext[HALO:HALO + h_rows, :] = h_new
    halo_copies = [
        remote(ext.at[h_rows:HALO + h_rows], ext.at[0:HALO], send_halo.at[0], recv_halo.at[0], at(above)),
        remote(ext.at[HALO:2 * HALO], ext.at[HALO + h_rows:2 * HALO + h_rows],
               send_halo.at[1], recv_halo.at[1], at(below)),
    ]
    h2_copies = [
        remote(h_next.at[mine], h_next.at[mine], send_h2.at[k], recv_h2.at[k], {"sig": sig_peer(k)})
        for k in range(1, n_sig)
    ]
    pending += halo_copies + h2_copies

    for copy in halo_copies:
        copy.wait_recv()
    signal = ext[...].astype(f32)
    length = signal.shape[0]
    position = index * h_rows - HALO + lax.broadcasted_iota(jnp.int32, signal.shape, 0)
    keep = (position >= 0) & (position < total * h_rows - 1)
    limit = jnp.where(keep, jnp.broadcast_to(tv_ref[...], signal.shape), 0.0)
    pull = TAU * (pltpu.roll(signal, length - 1, 0) - signal)

    def sweep(step, dual):
        around = pltpu.roll(dual, 1, 0) + pltpu.roll(dual, length - 1, 0)
        moved = pull + (1.0 - 2.0 * TAU) * dual + TAU * around
        return jnp.maximum(jnp.minimum(moved, limit), -limit)

    dual = lax.fori_loop(0, TV_STEPS, sweep, jnp.zeros_like(signal))
    smooth = signal - pltpu.roll(dual, 1, 0) + dual
    smooth_out[...] = smooth[HALO:HALO + h_rows, :]

    for copy in h2_copies:
        copy.wait_recv()
    part = jnp.zeros((8, w_blk.shape[1]), f32)
    for c in range(col_tiles):
        block = h_next[c * tile:(c + 1) * tile, :]
        h_tiles[1, c] = block
        part += block.astype(f32).reshape(tile // 8, 8, -1).sum(axis=0)
    row_part[build] = part
    rt_copies = [
        remote(row_part.at[build], row_part.at[build], send_rt.at[k], recv_rt.at[k], {"build": build_peer(k)})
        for k in range(1, n_build)
    ]
    pending += rt_copies

    def pass_w(step, carry):
        terms = []
        for g in range(GROUP):
            slot = step * GROUP + g
            h = h_tiles[1, meta[1, slot]]
            ratio = ratio_of(slot, w_tiles[meta[0, slot]], h)
            terms.append(jnp.dot(ratio, h, preferred_element_type=f32))
        for g in range(GROUP):
            slot = step * GROUP + g
            chain_w[slot + 1] = chain_w[meta[0, slots + slot]] + terms[g]
        return carry

    lax.fori_loop(0, slots // GROUP, pass_w, 0)
    for r in range(row_tiles):
        block = chain_w[meta[0, 2 * slots + r]]
        numer[r * tile:(r + 1) * tile, :] = block
        w_send[r * tile:(r + 1) * tile, :] = block.astype(bf16)
    nw_copies = [
        remote(w_send.at[rows_of(build_peer(k), w_rows)], w_recv.at[build], send_nw.at[k], recv_nw.at[k],
               {"build": build_peer(k)})
        for k in range(1, n_build)
    ]
    pending += nw_copies
    for copy in rt_copies:
        copy.wait_recv()
    row_sum = row_part[0]
    for k in range(1, n_build):
        row_sum += row_part[k]
    row_total = jnp.sum(row_sum, axis=0, keepdims=True)
    share = numer[rows_of(build, w_rows), :]
    for k in range(1, n_build):
        nw_copies[k - 1].wait_recv()
        share += w_recv[build_peer(n_build - k)].astype(f32)
    w_out[...] = (fw_ref[...].astype(f32) * share / row_total).astype(bf16)
    for copy in pending:
        copy.wait_send()


def links(index, tiles, count):
    slot = jnp.arange(index.shape[0], dtype=jnp.int32)
    same = (index[:, None] == index[None, :]) & (slot[None, :] < slot[:, None]) & (slot[None, :] < count)
    before = jnp.max(jnp.where(same, slot[None, :] + 1, 0), axis=1)
    hit = (jnp.arange(tiles, dtype=jnp.int32)[:, None] == index[None, :]) & (slot[None, :] < count)
    last = jnp.max(jnp.where(hit, slot[None, :] + 1, 0), axis=1)
    return jnp.concatenate([index, before, last])


def local(n_sig, n_build, tiles, tile_rows, tile_cols, tile_count, factor_w, factor_h, tv_weight):
    tiles = tiles[0, 0]
    slots, tile = tiles.shape[:2]
    w_rows, rank = factor_w.shape
    h_rows = factor_h.shape[0]
    block_rows, block_cols = w_rows * n_build, h_rows * n_sig
    most = max(block_rows, block_cols) // tile
    live = tile_count[0, 0]
    meta = jnp.stack([links(tile_rows[0, 0], most, live), links(tile_cols[0, 0], most, live)])
    vmem, smem = pltpu.VMEM, pltpu.SMEM
    f32, bf16 = jnp.float32, jnp.bfloat16
    dma = pltpu.SemaphoreType.DMA
    in_vmem = pl.BlockSpec(memory_space=pltpu.VMEM)
    in_smem = pl.BlockSpec(memory_space=pltpu.SMEM)
    return pl.pallas_call(
        functools.partial(kernel, n_sig, n_build),
        out_shape=(
            jax.ShapeDtypeStruct((w_rows, rank), bf16),
            jax.ShapeDtypeStruct((h_rows, rank), f32),
        ),
        in_specs=[in_smem, pl.BlockSpec(memory_space=pl.ANY), in_vmem, in_vmem, in_vmem],
        out_specs=(in_vmem, in_vmem),
        scratch_shapes=[
            vmem((slots, tile, tile), bf16),
            vmem((block_rows, rank), bf16),
            vmem((block_rows // tile, rank, tile), bf16),
            vmem((block_cols, rank), bf16),
            vmem((block_cols, rank), bf16),
            vmem((block_rows // tile, tile, rank), bf16),
            vmem((2, block_cols // tile, tile, rank), bf16),
            vmem((slots + 1, rank, tile), f32),
            vmem((slots + 1, tile, rank), f32),
            vmem((max(block_rows, block_cols), rank), f32),
            vmem((block_cols, rank), bf16),
            vmem((n_sig, h_rows, rank), bf16),
            vmem((block_rows, rank), bf16),
            vmem((n_build, w_rows, rank), bf16),
            vmem((n_sig, 8, rank), f32),
            vmem((n_build, 8, rank), f32),
            vmem((h_rows + 2 * HALO, rank), bf16),
            dma,
            dma((n_build,)), dma((n_build,)),
            dma((n_sig,)), dma((n_sig,)),
            dma((n_sig,)), dma((n_sig,)),
            dma((n_sig,)), dma((n_sig,)),
            dma((n_sig,)), dma((n_sig,)),
            dma((2,)), dma((2,)),
            dma((n_build,)), dma((n_build,)),
            dma((n_build,)), dma((n_build,)),
        ],
        compiler_params=pltpu.CompilerParams(
            collective_id=0, has_side_effects=True, vmem_limit_bytes=40 * 1024 * 1024
        ),
    )(meta, tiles, factor_w, factor_h, tv_weight[None, :])


def solution(mesh):
    return jax.shard_map(
        functools.partial(local, mesh.shape["sig"], mesh.shape["build"]),
        mesh=mesh,
        in_specs=(
            P(("groups", "sig"), "build", None, None, None),
            P(("groups", "sig"), "build", None),
            P(("groups", "sig"), "build", None),
            P(("groups", "sig"), "build"),
            P(("groups", "sig", "build"), None),
            P(("groups", "sig", "build"), None),
            P("groups"),
        ),
        out_specs=(P(("groups", "sig", "build"), None), P(("groups", "sig", "build"), None)),
        check_vma=False,
    )
```

```python
import functools

import jax
import jax.numpy as jnp
from jax import lax
from jax.experimental import pallas as pl
from jax.experimental.pallas import tpu as pltpu
from jax.sharding import PartitionSpec as P

TV_STEPS = 16
TAU = 0.25
HALO = 32
GROUP = 8
MESH = pl.DeviceIdType.MESH


def kernel(
    n_sig, n_build,
    rows_hbm, cols_hbm, count, tiles_hbm, fw_hbm, fh_hbm, tv_ref,
    w_out, smooth_out,
    tiles, w_blk, w_turn, h_blk, h_next, w_tiles, h_tiles, chain_h, chain_w, numer,
    h_send, h_recv, w_send, w_recv, col_part, row_part, ext,
    fw_ref, fh_ref, index_ref, link_ref, meta, tile_sem, local_sem, send_w, recv_w, send_h, recv_h, send_ct, recv_ct, send_nh, recv_nh,
    send_h2, recv_h2, send_halo, recv_halo, send_rt, recv_rt, send_nw, recv_nw,
):
    f32, bf16 = jnp.float32, jnp.bfloat16
    sig = lax.axis_index("sig")
    build = lax.axis_index("build")
    slots, tile = tiles.shape[0], tiles.shape[1]
    w_rows, h_rows = fw_ref.shape[0], fh_ref.shape[0]
    row_tiles = w_blk.shape[0] // tile
    col_tiles = h_blk.shape[0] // tile

    load = pltpu.make_async_copy(tiles_hbm, tiles, tile_sem)
    load.start()
    local_copies = [
        pltpu.make_async_copy(src, dst, local_sem.at[i])
        for i, (src, dst) in enumerate([
            (fw_hbm, fw_ref), (fh_hbm, fh_ref),
            (rows_hbm, index_ref.at[0]), (cols_hbm, index_ref.at[1]),
        ])
    ]
    for copy in local_copies:
        copy.start()

    def sig_peer(k):
        return lax.rem(sig + k, n_sig)

    def build_peer(k):
        return lax.rem(build + k, n_build)

    total = n_sig * n_build
    index = sig * n_build + build
    above = lax.rem(index + 1, total)
    below = lax.rem(index + total - 1, total)

    def at(linear):
        return {"sig": lax.div(linear, n_build), "build": lax.rem(linear, n_build)}

    barrier = pltpu.get_barrier_semaphore()
    for k in range(1, n_sig):
        pl.semaphore_signal(barrier, inc=1, device_id={"sig": sig_peer(k)}, device_id_type=MESH)
    for k in range(1, n_build):
        pl.semaphore_signal(barrier, inc=1, device_id={"build": build_peer(k)}, device_id_type=MESH)
    pl.semaphore_signal(barrier, inc=1, device_id=at(above), device_id_type=MESH)
    pl.semaphore_signal(barrier, inc=1, device_id=at(below), device_id_type=MESH)
    pl.semaphore_wait(barrier, n_sig + n_build)

    def remote(src, dst, send, recv, device):
        copy = pltpu.make_async_remote_copy(
            src_ref=src, dst_ref=dst, send_sem=send, recv_sem=recv,
            device_id=device, device_id_type=MESH,
        )
        copy.start()
        return copy

    def rows_of(place, rows):
        return pl.ds(pl.multiple_of(place * rows, rows), rows)

    pending = []

    h_copies = [
        remote(fh_hbm, h_blk.at[rows_of(sig, h_rows)], send_h.at[k], recv_h.at[k], {"sig": sig_peer(k)})
        for k in range(1, n_sig)
    ]
    w_copies = [
        remote(fw_hbm, w_blk.at[rows_of(build, w_rows)], send_w.at[k], recv_w.at[k], {"build": build_peer(k)})
        for k in range(1, n_build)
    ]
    pending += h_copies + w_copies
    for copy in local_copies:
        copy.wait()
    live = count[0, 0]
    down = lax.broadcasted_iota(jnp.int32, (slots, slots), 0)
    along = lax.broadcasted_iota(jnp.int32, (slots, slots), 1)
    for side in range(2):
        index_row = jnp.broadcast_to(index_ref[side], (slots, slots))
        index_col = jnp.sum(jnp.where(down == along, index_row, 0), axis=1, keepdims=True)
        index_col = jnp.broadcast_to(index_col, (slots, slots))
        same = (index_col == index_row) & (down < along) & (down < live)
        hit = (index_col == along) & (down < live)
        lines = [
            index_row[:1],
            jnp.max(jnp.where(same, down + 1, 0), axis=0, keepdims=True),
            jnp.max(jnp.where(hit, down + 1, 0), axis=0, keepdims=True),
        ]
        for i, line in enumerate(lines):
            link_ref[3 * side + i:3 * side + i + 1, 0:slots] = line
    link_copy = pltpu.make_async_copy(link_ref, meta, local_sem.at[4])
    link_copy.start()

    def link(line, place, most):
        return jnp.clip(meta[line, place], 0, most)

    h_blk[rows_of(sig, h_rows), :] = fh_ref[...]
    w_blk[rows_of(build, w_rows), :] = fw_ref[...]
    chain_h[0] = jnp.zeros(chain_h.shape[1:], f32)
    chain_w[0] = jnp.zeros(chain_w.shape[1:], f32)

    for copy in w_copies:
        copy.wait_recv()
    part = jnp.zeros((8, w_blk.shape[1]), f32)
    for r in range(row_tiles):
        block = w_blk[r * tile:(r + 1) * tile, :]
        w_tiles[r] = block
        w_turn[r] = block.T
        part += block.astype(f32).reshape(tile // 8, 8, -1).sum(axis=0)
    col_part[sig] = part
    ct_copies = [
        remote(col_part.at[sig], col_part.at[sig], send_ct.at[k], recv_ct.at[k], {"sig": sig_peer(k)})
        for k in range(1, n_sig)
    ]
    pending += ct_copies

    load.wait()
    link_copy.wait()
    for copy in h_copies:
        copy.wait_recv()
    for c in range(col_tiles):
        h_tiles[0, c] = h_blk[c * tile:(c + 1) * tile, :]

    def ratio_of(slot, w, h):
        product = lax.dot_general(w, h, (((1,), (1,)), ((), ())), preferred_element_type=f32)
        return (tiles[slot].astype(f32) / product).astype(bf16)

    def pass_h(step, carry):
        terms = []
        for g in range(GROUP):
            slot = step * GROUP + g
            row, col = link(0, slot, row_tiles - 1), link(3, slot, col_tiles - 1)
            ratio = ratio_of(slot, w_tiles[row], h_tiles[0, col])
            terms.append(jnp.dot(w_turn[row], ratio, preferred_element_type=f32))
        for g in range(GROUP):
            slot = step * GROUP + g
            chain_h[slot + 1] = chain_h[link(4, slot, slots)] + terms[g]
        return carry

    lax.fori_loop(0, slots // GROUP, pass_h, 0)
    for c in range(col_tiles):
        block = chain_h[link(5, c, slots)].T
        numer[c * tile:(c + 1) * tile, :] = block
        h_send[c * tile:(c + 1) * tile, :] = block.astype(bf16)
    nh_copies = [
        remote(h_send.at[rows_of(sig_peer(k), h_rows)], h_recv.at[sig], send_nh.at[k], recv_nh.at[k],
               {"sig": sig_peer(k)})
        for k in range(1, n_sig)
    ]
    pending += nh_copies
    for copy in ct_copies:
        copy.wait_recv()
    col_sum = col_part[0]
    for k in range(1, n_sig):
        col_sum += col_part[k]
    col_total = jnp.sum(col_sum, axis=0, keepdims=True)
    share = numer[rows_of(sig, h_rows), :]
    for k in range(1, n_sig):
        nh_copies[k - 1].wait_recv()
        share += h_recv[sig_peer(n_sig - k)].astype(f32)
    h_new = (fh_ref[...].astype(f32) * share / col_total).astype(bf16)
    mine = rows_of(sig, h_rows)
    h_next[mine, :] = h_new
    ext[HALO:HALO + h_rows, :] = h_new
    halo_copies = [
        remote(ext.at[h_rows:HALO + h_rows], ext.at[0:HALO], send_halo.at[0], recv_halo.at[0], at(above)),
        remote(ext.at[HALO:2 * HALO], ext.at[HALO + h_rows:2 * HALO + h_rows],
               send_halo.at[1], recv_halo.at[1], at(below)),
    ]
    h2_copies = [
        remote(h_next.at[mine], h_next.at[mine], send_h2.at[k], recv_h2.at[k], {"sig": sig_peer(k)})
        for k in range(1, n_sig)
    ]
    pending += halo_copies + h2_copies

    for copy in halo_copies:
        copy.wait_recv()
    signal = ext[...].astype(f32)
    length = signal.shape[0]
    position = index * h_rows - HALO + lax.broadcasted_iota(jnp.int32, signal.shape, 0)
    keep = (position >= 0) & (position < total * h_rows - 1)
    limit = jnp.where(keep, jnp.broadcast_to(tv_ref[...], signal.shape), 0.0)
    pull = TAU * (pltpu.roll(signal, length - 1, 0) - signal)

    def sweep(step, dual):
        around = pltpu.roll(dual, 1, 0) + pltpu.roll(dual, length - 1, 0)
        moved = pull + (1.0 - 2.0 * TAU) * dual + TAU * around
        return jnp.maximum(jnp.minimum(moved, limit), -limit)

    dual = lax.fori_loop(0, TV_STEPS, sweep, jnp.zeros_like(signal))
    smooth = signal - pltpu.roll(dual, 1, 0) + dual
    smooth_out[...] = smooth[HALO:HALO + h_rows, :]

    for copy in h2_copies:
        copy.wait_recv()
    part = jnp.zeros((8, w_blk.shape[1]), f32)
    for c in range(col_tiles):
        block = h_next[c * tile:(c + 1) * tile, :]
        h_tiles[1, c] = block
        part += block.astype(f32).reshape(tile // 8, 8, -1).sum(axis=0)
    row_part[build] = part
    rt_copies = [
        remote(row_part.at[build], row_part.at[build], send_rt.at[k], recv_rt.at[k], {"build": build_peer(k)})
        for k in range(1, n_build)
    ]
    pending += rt_copies

    def pass_w(step, carry):
        terms = []
        for g in range(GROUP):
            slot = step * GROUP + g
            h = h_tiles[1, link(3, slot, col_tiles - 1)]
            ratio = ratio_of(slot, w_tiles[link(0, slot, row_tiles - 1)], h)
            terms.append(jnp.dot(ratio, h, preferred_element_type=f32))
        for g in range(GROUP):
            slot = step * GROUP + g
            chain_w[slot + 1] = chain_w[link(1, slot, slots)] + terms[g]
        return carry

    lax.fori_loop(0, slots // GROUP, pass_w, 0)
    for r in range(row_tiles):
        block = chain_w[link(2, r, slots)]
        numer[r * tile:(r + 1) * tile, :] = block
        w_send[r * tile:(r + 1) * tile, :] = block.astype(bf16)
    nw_copies = [
        remote(w_send.at[rows_of(build_peer(k), w_rows)], w_recv.at[build], send_nw.at[k], recv_nw.at[k],
               {"build": build_peer(k)})
        for k in range(1, n_build)
    ]
    pending += nw_copies
    for copy in rt_copies:
        copy.wait_recv()
    row_sum = row_part[0]
    for k in range(1, n_build):
        row_sum += row_part[k]
    row_total = jnp.sum(row_sum, axis=0, keepdims=True)
    share = numer[rows_of(build, w_rows), :]
    for k in range(1, n_build):
        nw_copies[k - 1].wait_recv()
        share += w_recv[build_peer(n_build - k)].astype(f32)
    w_out[...] = (fw_ref[...].astype(f32) * share / row_total).astype(bf16)
    for copy in pending:
        copy.wait_send()


def local(n_sig, n_build, tiles, tile_rows, tile_cols, tile_count, factor_w, factor_h, tv_weight):
    tiles = tiles[0, 0]
    slots, tile = tiles.shape[:2]
    w_rows, rank = factor_w.shape
    h_rows = factor_h.shape[0]
    block_rows, block_cols = w_rows * n_build, h_rows * n_sig
    vmem, smem = pltpu.VMEM, pltpu.SMEM
    f32, bf16 = jnp.float32, jnp.bfloat16
    dma = pltpu.SemaphoreType.DMA
    in_vmem = pl.BlockSpec(memory_space=pltpu.VMEM)
    in_hbm = pl.BlockSpec(memory_space=pltpu.HBM)
    in_smem = pl.BlockSpec(memory_space=pltpu.SMEM)
    return pl.pallas_call(
        functools.partial(kernel, n_sig, n_build),
        out_shape=(
            jax.ShapeDtypeStruct((w_rows, rank), bf16),
            jax.ShapeDtypeStruct((h_rows, rank), f32),
        ),
        in_specs=[in_hbm, in_hbm, in_smem, in_hbm, in_hbm, in_hbm, in_vmem],
        out_specs=(in_vmem, in_vmem),
        scratch_shapes=[
            vmem((slots, tile, tile), bf16),
            vmem((block_rows, rank), bf16),
            vmem((block_rows // tile, rank, tile), bf16),
            vmem((block_cols, rank), bf16),
            vmem((block_cols, rank), bf16),
            vmem((block_rows // tile, tile, rank), bf16),
            vmem((2, block_cols // tile, tile, rank), bf16),
            vmem((slots + 1, rank, tile), f32),
            vmem((slots + 1, tile, rank), f32),
            vmem((max(block_rows, block_cols), rank), f32),
            vmem((block_cols, rank), bf16),
            vmem((n_sig, h_rows, rank), bf16),
            vmem((block_rows, rank), bf16),
            vmem((n_build, w_rows, rank), bf16),
            vmem((n_sig, 8, rank), f32),
            vmem((n_build, 8, rank), f32),
            vmem((h_rows + 2 * HALO, rank), bf16),
            vmem((w_rows, rank), bf16),
            vmem((h_rows, rank), bf16),
            vmem((2, 1, slots), jnp.int32),
            vmem((8, 128), jnp.int32),
            smem((8, 128), jnp.int32),
            dma, dma((5,)),
            dma((n_build,)), dma((n_build,)),
            dma((n_sig,)), dma((n_sig,)),
            dma((n_sig,)), dma((n_sig,)),
            dma((n_sig,)), dma((n_sig,)),
            dma((n_sig,)), dma((n_sig,)),
            dma((2,)), dma((2,)),
            dma((n_build,)), dma((n_build,)),
            dma((n_build,)), dma((n_build,)),
        ],
        compiler_params=pltpu.CompilerParams(
            collective_id=0, has_side_effects=True, vmem_limit_bytes=60 * 1024 * 1024
        ),
    )(tile_rows[0], tile_cols[0], tile_count, tiles, factor_w, factor_h, tv_weight[None, :])


def solution(mesh):
    return jax.shard_map(
        functools.partial(local, mesh.shape["sig"], mesh.shape["build"]),
        mesh=mesh,
        in_specs=(
            P(("groups", "sig"), "build", None, None, None),
            P(("groups", "sig"), "build", None),
            P(("groups", "sig"), "build", None),
            P(("groups", "sig"), "build"),
            P(("groups", "sig", "build"), None),
            P(("groups", "sig", "build"), None),
            P("groups"),
        ),
        out_specs=(P(("groups", "sig", "build"), None), P(("groups", "sig", "build"), None)),
        check_vma=False,
    )
```

```python
import functools

import jax
import jax.numpy as jnp
from jax import lax
from jax.experimental import pallas as pl
from jax.experimental.pallas import tpu as pltpu
from jax.sharding import PartitionSpec as P

TV_STEPS = 16
TAU = 0.25
HALO = 32
GROUP = 8
MESH = pl.DeviceIdType.MESH


def kernel(
    n_sig, n_build,
    rows_hbm, cols_hbm, count, tiles_hbm, fw_hbm, fh_hbm, tv_ref,
    w_out, smooth_out,
    tiles, w_blk, w_turn, h_blk, h_next, w_tiles, h_tiles, chain_h, chain_w, numer,
    h_send, h_recv, w_send, w_recv, col_part, row_part, ext,
    fw_ref, fh_ref, index_ref, link_ref, meta, h_hop, send_on, recv_hop, tile_sem, local_sem, send_w, recv_w, send_h, recv_h, send_ct, recv_ct, send_nh, recv_nh,
    send_h2, recv_h2, send_halo, recv_halo, send_rt, recv_rt, send_nw, recv_nw,
):
    f32, bf16 = jnp.float32, jnp.bfloat16
    sig = lax.axis_index("sig")
    build = lax.axis_index("build")
    slots, tile = tiles.shape[0], tiles.shape[1]
    w_rows, h_rows = fw_ref.shape[0], fh_ref.shape[0]
    row_tiles = w_blk.shape[0] // tile
    col_tiles = h_blk.shape[0] // tile

    load = pltpu.make_async_copy(tiles_hbm, tiles, tile_sem)
    load.start()
    local_copies = [
        pltpu.make_async_copy(src, dst, local_sem.at[i])
        for i, (src, dst) in enumerate([
            (fw_hbm, fw_ref), (fh_hbm, fh_ref),
            (rows_hbm, index_ref.at[0]), (cols_hbm, index_ref.at[1]),
        ])
    ]
    for copy in local_copies:
        copy.start()

    def sig_peer(k):
        return lax.rem(sig + k, n_sig)

    def build_peer(k):
        return lax.rem(build + k, n_build)

    total = n_sig * n_build
    index = sig * n_build + build
    above = lax.rem(index + 1, total)
    below = lax.rem(index + total - 1, total)

    def at(linear):
        return {"sig": lax.div(linear, n_build), "build": lax.rem(linear, n_build)}

    barrier = pltpu.get_barrier_semaphore()
    for k in range(1, n_sig):
        pl.semaphore_signal(barrier, inc=1, device_id={"sig": sig_peer(k)}, device_id_type=MESH)
    for k in range(1, n_build):
        pl.semaphore_signal(barrier, inc=1, device_id={"build": build_peer(k)}, device_id_type=MESH)
    pl.semaphore_signal(barrier, inc=1, device_id=at(above), device_id_type=MESH)
    pl.semaphore_signal(barrier, inc=1, device_id=at(below), device_id_type=MESH)
    pl.semaphore_wait(barrier, n_sig + n_build)

    def describe(src, dst, send, recv, device):
        return pltpu.make_async_remote_copy(
            src_ref=src, dst_ref=dst, send_sem=send, recv_sem=recv,
            device_id=device, device_id_type=MESH,
        )

    def remote(src, dst, send, recv, device):
        copy = describe(src, dst, send, recv, device)
        copy.start()
        return copy

    def rows_of(place, rows):
        return pl.ds(pl.multiple_of(place * rows, rows), rows)

    pending = []
    relay = n_sig == 4
    order = [2, 1, 3] if relay else list(range(1, n_sig))
    is_end = (sig == 0) | (sig == n_sig - 1)
    far = n_sig - 1 - sig
    inner = jnp.where(sig * 2 < n_sig, 1, n_sig - 2)
    outer = jnp.where(sig * 2 < n_sig, 0, n_sig - 1)

    def when(condition, action):
        if condition is None:
            action()
        else:
            pl.when(condition)(action)

    def sends(k):
        if not relay or k == 2:
            return None
        return sig != (0 if k == n_sig - 1 else n_sig - 1)

    class Gather:
        def __init__(self, src, block, send, recv, send_on):
            mine = block.at[rows_of(sig, h_rows)]
            self.copies = {
                k: describe(src, mine, send.at[k], recv.at[k], {"sig": sig_peer(k)}) for k in order
            }
            for k in order:
                when(sends(k), self.copies[k].start)
            crossed = block.at[rows_of(sig_peer(2), h_rows)]
            self.on = [
                describe(crossed, crossed, send_on, recv.at[k], {"sig": outer}) for k in (1, n_sig - 1)
            ] if relay else []

        def receive(self):
            for k in order:
                self.copies[k].wait_recv()
                if relay and k == 2:
                    when(sig == 1, self.on[0].start)
                    when(sig == n_sig - 2, self.on[1].start)

        def finish(self):
            for k in order:
                when(sends(k), self.copies[k].wait_send)
            if relay:
                when(sig == 1, self.on[0].wait_send)
                when(sig == n_sig - 2, self.on[1].wait_send)

    gather_h = Gather(fh_hbm, h_blk, send_h, recv_h, send_on.at[0])
    w_copies = [
        remote(fw_hbm, w_blk.at[rows_of(build, w_rows)], send_w.at[k], recv_w.at[k], {"build": build_peer(k)})
        for k in range(1, n_build)
    ]
    pending += w_copies
    for copy in local_copies:
        copy.wait()
    live = count[0, 0]
    down = lax.broadcasted_iota(jnp.int32, (slots, slots), 0)
    along = lax.broadcasted_iota(jnp.int32, (slots, slots), 1)
    for side in range(2):
        index_row = jnp.broadcast_to(index_ref[side], (slots, slots))
        index_col = jnp.sum(jnp.where(down == along, index_row, 0), axis=1, keepdims=True)
        index_col = jnp.broadcast_to(index_col, (slots, slots))
        same = (index_col == index_row) & (down < along) & (down < live)
        hit = (index_col == along) & (down < live)
        lines = [
            index_row[:1],
            jnp.max(jnp.where(same, down + 1, 0), axis=0, keepdims=True),
            jnp.max(jnp.where(hit, down + 1, 0), axis=0, keepdims=True),
        ]
        for i, line in enumerate(lines):
            link_ref[3 * side + i:3 * side + i + 1, 0:slots] = line
    link_copy = pltpu.make_async_copy(link_ref, meta, local_sem.at[4])
    link_copy.start()

    def link(line, place, most):
        return jnp.clip(meta[line, place], 0, most)

    h_blk[rows_of(sig, h_rows), :] = fh_ref[...]
    w_blk[rows_of(build, w_rows), :] = fw_ref[...]
    chain_h[0] = jnp.zeros(chain_h.shape[1:], f32)
    chain_w[0] = jnp.zeros(chain_w.shape[1:], f32)

    for copy in w_copies:
        copy.wait_recv()
    part = jnp.zeros((8, w_blk.shape[1]), f32)
    for r in range(row_tiles):
        block = w_blk[r * tile:(r + 1) * tile, :]
        w_tiles[r] = block
        w_turn[r] = block.T
        part += block.astype(f32).reshape(tile // 8, 8, -1).sum(axis=0)
    col_part[sig] = part
    ct_copies = [
        remote(col_part.at[sig], col_part.at[sig], send_ct.at[k], recv_ct.at[k], {"sig": sig_peer(k)})
        for k in range(1, n_sig)
    ]
    pending += ct_copies

    load.wait()
    link_copy.wait()
    gather_h.receive()
    for c in range(col_tiles):
        h_tiles[0, c] = h_blk[c * tile:(c + 1) * tile, :]

    def ratio_of(slot, w, h):
        product = lax.dot_general(w, h, (((1,), (1,)), ((), ())), preferred_element_type=f32)
        return (tiles[slot].astype(f32) / product).astype(bf16)

    def pass_h(step, carry):
        terms = []
        for g in range(GROUP):
            slot = step * GROUP + g
            row, col = link(0, slot, row_tiles - 1), link(3, slot, col_tiles - 1)
            ratio = ratio_of(slot, w_tiles[row], h_tiles[0, col])
            terms.append(jnp.dot(w_turn[row], ratio, preferred_element_type=f32))
        for g in range(GROUP):
            slot = step * GROUP + g
            chain_h[slot + 1] = chain_h[link(4, slot, slots)] + terms[g]
        return carry

    lax.fori_loop(0, slots // GROUP, pass_h, 0)
    for c in range(col_tiles):
        block = chain_h[link(5, c, slots)].T
        numer[c * tile:(c + 1) * tile, :] = block
        h_send[c * tile:(c + 1) * tile, :] = block.astype(bf16)
    nh_copies = {
        k: describe(h_send.at[rows_of(sig_peer(k), h_rows)], h_recv.at[sig], send_nh.at[k], recv_nh.at[k],
                    {"sig": sig_peer(k)})
        for k in order
    }
    hop = describe(h_send.at[rows_of(far, h_rows)], h_hop, send_on.at[2], recv_hop, {"sig": inner})
    if relay:
        when(is_end, hop.start)
    for k in order:
        when(is_end if relay and k == 2 else sends(k), nh_copies[k].start)
    if relay:
        @pl.when(jnp.logical_not(is_end))
        def _():
            hop.wait_recv()
            crossing = rows_of(sig_peer(2), h_rows)
            h_send[crossing, :] = (numer[crossing, :] + h_hop[...].astype(f32)).astype(bf16)
            nh_copies[2].start()
    for copy in ct_copies:
        copy.wait_recv()
    col_sum = col_part[0]
    for k in range(1, n_sig):
        col_sum += col_part[k]
    col_total = jnp.sum(col_sum, axis=0, keepdims=True)
    mine = rows_of(sig, h_rows)

    def add(k):
        nh_copies[k].wait_recv()
        numer[mine, :] += h_recv[sig_peer(n_sig - k)].astype(f32)

    for k in order[::-1]:
        arrives = None if not relay or k == 2 else sig != (n_sig - 1 if k == n_sig - 1 else 0)
        when(arrives, functools.partial(add, k))
    share = numer[mine, :]
    h_new = (fh_ref[...].astype(f32) * share / col_total).astype(bf16)
    h_next[mine, :] = h_new
    ext[HALO:HALO + h_rows, :] = h_new
    halo_copies = [
        remote(ext.at[h_rows:HALO + h_rows], ext.at[0:HALO], send_halo.at[0], recv_halo.at[0], at(above)),
        remote(ext.at[HALO:2 * HALO], ext.at[HALO + h_rows:2 * HALO + h_rows],
               send_halo.at[1], recv_halo.at[1], at(below)),
    ]
    gather_next = Gather(h_next.at[mine], h_next, send_h2, recv_h2, send_on.at[1])
    pending += halo_copies

    for copy in halo_copies:
        copy.wait_recv()
    signal = ext[...].astype(f32)
    length = signal.shape[0]
    position = index * h_rows - HALO + lax.broadcasted_iota(jnp.int32, signal.shape, 0)
    keep = (position >= 0) & (position < total * h_rows - 1)
    limit = jnp.where(keep, jnp.broadcast_to(tv_ref[...], signal.shape), 0.0)
    pull = TAU * (pltpu.roll(signal, length - 1, 0) - signal)

    def sweep(step, dual):
        around = pltpu.roll(dual, 1, 0) + pltpu.roll(dual, length - 1, 0)
        moved = pull + (1.0 - 2.0 * TAU) * dual + TAU * around
        return jnp.maximum(jnp.minimum(moved, limit), -limit)

    dual = lax.fori_loop(0, TV_STEPS, sweep, jnp.zeros_like(signal))
    smooth = signal - pltpu.roll(dual, 1, 0) + dual
    smooth_out[...] = smooth[HALO:HALO + h_rows, :]

    gather_next.receive()
    part = jnp.zeros((8, w_blk.shape[1]), f32)
    for c in range(col_tiles):
        block = h_next[c * tile:(c + 1) * tile, :]
        h_tiles[1, c] = block
        part += block.astype(f32).reshape(tile // 8, 8, -1).sum(axis=0)
    row_part[build] = part
    rt_copies = [
        remote(row_part.at[build], row_part.at[build], send_rt.at[k], recv_rt.at[k], {"build": build_peer(k)})
        for k in range(1, n_build)
    ]
    pending += rt_copies

    def pass_w(step, carry):
        terms = []
        for g in range(GROUP):
            slot = step * GROUP + g
            h = h_tiles[1, link(3, slot, col_tiles - 1)]
            ratio = ratio_of(slot, w_tiles[link(0, slot, row_tiles - 1)], h)
            terms.append(jnp.dot(ratio, h, preferred_element_type=f32))
        for g in range(GROUP):
            slot = step * GROUP + g
            chain_w[slot + 1] = chain_w[link(1, slot, slots)] + terms[g]
        return carry

    lax.fori_loop(0, slots // GROUP, pass_w, 0)
    for r in range(row_tiles):
        block = chain_w[link(2, r, slots)]
        numer[r * tile:(r + 1) * tile, :] = block
        w_send[r * tile:(r + 1) * tile, :] = block.astype(bf16)
    nw_copies = [
        remote(w_send.at[rows_of(build_peer(k), w_rows)], w_recv.at[build], send_nw.at[k], recv_nw.at[k],
               {"build": build_peer(k)})
        for k in range(1, n_build)
    ]
    pending += nw_copies
    for copy in rt_copies:
        copy.wait_recv()
    row_sum = row_part[0]
    for k in range(1, n_build):
        row_sum += row_part[k]
    row_total = jnp.sum(row_sum, axis=0, keepdims=True)
    share = numer[rows_of(build, w_rows), :]
    for k in range(1, n_build):
        nw_copies[k - 1].wait_recv()
        share += w_recv[build_peer(n_build - k)].astype(f32)
    w_out[...] = (fw_ref[...].astype(f32) * share / row_total).astype(bf16)
    for copy in pending:
        copy.wait_send()
    gather_h.finish()
    gather_next.finish()
    for k in order:
        when(sends(k), nh_copies[k].wait_send)
    if relay:
        when(is_end, hop.wait_send)


def local(n_sig, n_build, tiles, tile_rows, tile_cols, tile_count, factor_w, factor_h, tv_weight):
    tiles = tiles[0, 0]
    slots, tile = tiles.shape[:2]
    w_rows, rank = factor_w.shape
    h_rows = factor_h.shape[0]
    block_rows, block_cols = w_rows * n_build, h_rows * n_sig
    vmem, smem = pltpu.VMEM, pltpu.SMEM
    f32, bf16 = jnp.float32, jnp.bfloat16
    dma = pltpu.SemaphoreType.DMA
    in_vmem = pl.BlockSpec(memory_space=pltpu.VMEM)
    in_hbm = pl.BlockSpec(memory_space=pltpu.HBM)
    in_smem = pl.BlockSpec(memory_space=pltpu.SMEM)
    return pl.pallas_call(
        functools.partial(kernel, n_sig, n_build),
        out_shape=(
            jax.ShapeDtypeStruct((w_rows, rank), bf16),
            jax.ShapeDtypeStruct((h_rows, rank), f32),
        ),
        in_specs=[in_hbm, in_hbm, in_smem, in_hbm, in_hbm, in_hbm, in_vmem],
        out_specs=(in_vmem, in_vmem),
        scratch_shapes=[
            vmem((slots, tile, tile), bf16),
            vmem((block_rows, rank), bf16),
            vmem((block_rows // tile, rank, tile), bf16),
            vmem((block_cols, rank), bf16),
            vmem((block_cols, rank), bf16),
            vmem((block_rows // tile, tile, rank), bf16),
            vmem((2, block_cols // tile, tile, rank), bf16),
            vmem((slots + 1, rank, tile), f32),
            vmem((slots + 1, tile, rank), f32),
            vmem((max(block_rows, block_cols), rank), f32),
            vmem((block_cols, rank), bf16),
            vmem((n_sig, h_rows, rank), bf16),
            vmem((block_rows, rank), bf16),
            vmem((n_build, w_rows, rank), bf16),
            vmem((n_sig, 8, rank), f32),
            vmem((n_build, 8, rank), f32),
            vmem((h_rows + 2 * HALO, rank), bf16),
            vmem((w_rows, rank), bf16),
            vmem((h_rows, rank), bf16),
            vmem((2, 1, slots), jnp.int32),
            vmem((8, 128), jnp.int32),
            smem((8, 128), jnp.int32),
            vmem((h_rows, rank), bf16),
            dma((3,)), dma,
            dma, dma((5,)),
            dma((n_build,)), dma((n_build,)),
            dma((n_sig,)), dma((n_sig,)),
            dma((n_sig,)), dma((n_sig,)),
            dma((n_sig,)), dma((n_sig,)),
            dma((n_sig,)), dma((n_sig,)),
            dma((2,)), dma((2,)),
            dma((n_build,)), dma((n_build,)),
            dma((n_build,)), dma((n_build,)),
        ],
        compiler_params=pltpu.CompilerParams(
            collective_id=0, has_side_effects=True, vmem_limit_bytes=60 * 1024 * 1024
        ),
    )(tile_rows[0], tile_cols[0], tile_count, tiles, factor_w, factor_h, tv_weight[None, :])


def solution(mesh):
    return jax.shard_map(
        functools.partial(local, mesh.shape["sig"], mesh.shape["build"]),
        mesh=mesh,
        in_specs=(
            P(("groups", "sig"), "build", None, None, None),
            P(("groups", "sig"), "build", None),
            P(("groups", "sig"), "build", None),
            P(("groups", "sig"), "build"),
            P(("groups", "sig", "build"), None),
            P(("groups", "sig", "build"), None),
            P("groups"),
        ),
        out_specs=(P(("groups", "sig", "build"), None), P(("groups", "sig", "build"), None)),
        check_vma=False,
    )
```

```python
import functools

import jax
import jax.numpy as jnp
from jax import lax
from jax.experimental import pallas as pl
from jax.experimental.pallas import tpu as pltpu
from jax.sharding import PartitionSpec as P

TV_STEPS = 16
TAU = 0.25
HALO = 32
GROUP = 16
MESH = pl.DeviceIdType.MESH


def kernel(
    n_sig, n_build,
    rows_hbm, cols_hbm, count, tiles_hbm, fw_hbm, fh_hbm, tv_ref,
    w_out, smooth_out,
    tiles, w_blk, w_turn, h_blk, h_next, w_tiles, h_tiles, chain_h, chain_w, numer,
    h_send, h_recv, w_send, w_recv, col_part, row_part, ext,
    fw_ref, fh_ref, index_ref, link_ref, meta, h_hop, send_on, recv_hop, tile_sem, local_sem, send_w, recv_w, send_h, recv_h, send_ct, recv_ct, send_nh, recv_nh,
    send_h2, recv_h2, send_halo, recv_halo, send_rt, recv_rt, send_nw, recv_nw,
):
    f32, bf16 = jnp.float32, jnp.bfloat16
    sig = lax.axis_index("sig")
    build = lax.axis_index("build")
    slots, tile = tiles.shape[0], tiles.shape[1]
    w_rows, h_rows = fw_ref.shape[0], fh_ref.shape[0]
    row_tiles = w_blk.shape[0] // tile
    col_tiles = h_blk.shape[0] // tile

    load = pltpu.make_async_copy(tiles_hbm, tiles, tile_sem)
    load.start()
    local_copies = [
        pltpu.make_async_copy(src, dst, local_sem.at[i])
        for i, (src, dst) in enumerate([
            (fw_hbm, fw_ref), (fh_hbm, fh_ref),
            (rows_hbm, index_ref.at[0]), (cols_hbm, index_ref.at[1]),
        ])
    ]
    for copy in local_copies:
        copy.start()

    def sig_peer(k):
        return lax.rem(sig + k, n_sig)

    def build_peer(k):
        return lax.rem(build + k, n_build)

    total = n_sig * n_build
    index = sig * n_build + build
    above = lax.rem(index + 1, total)
    below = lax.rem(index + total - 1, total)

    def at(linear):
        return {"sig": lax.div(linear, n_build), "build": lax.rem(linear, n_build)}

    barrier = pltpu.get_barrier_semaphore()
    for k in range(1, n_sig):
        pl.semaphore_signal(barrier, inc=1, device_id={"sig": sig_peer(k)}, device_id_type=MESH)
    for k in range(1, n_build):
        pl.semaphore_signal(barrier, inc=1, device_id={"build": build_peer(k)}, device_id_type=MESH)
    pl.semaphore_signal(barrier, inc=1, device_id=at(above), device_id_type=MESH)
    pl.semaphore_signal(barrier, inc=1, device_id=at(below), device_id_type=MESH)
    pl.semaphore_wait(barrier, n_sig + n_build)

    def describe(src, dst, send, recv, device):
        return pltpu.make_async_remote_copy(
            src_ref=src, dst_ref=dst, send_sem=send, recv_sem=recv,
            device_id=device, device_id_type=MESH,
        )

    def remote(src, dst, send, recv, device):
        copy = describe(src, dst, send, recv, device)
        copy.start()
        return copy

    def rows_of(place, rows):
        return pl.ds(pl.multiple_of(place * rows, rows), rows)

    pending = []
    relay = n_sig == 4
    order = [2, 1, 3] if relay else list(range(1, n_sig))
    is_end = (sig == 0) | (sig == n_sig - 1)
    far = n_sig - 1 - sig
    inner = jnp.where(sig * 2 < n_sig, 1, n_sig - 2)
    outer = jnp.where(sig * 2 < n_sig, 0, n_sig - 1)

    def when(condition, action):
        if condition is None:
            action()
        else:
            pl.when(condition)(action)

    def sends(k):
        if not relay or k == 2:
            return None
        return sig != (0 if k == n_sig - 1 else n_sig - 1)

    class Gather:
        def __init__(self, src, block, send, recv, send_on):
            mine = block.at[rows_of(sig, h_rows)]
            self.copies = {
                k: describe(src, mine, send.at[k], recv.at[k], {"sig": sig_peer(k)}) for k in order
            }
            for k in order:
                when(sends(k), self.copies[k].start)
            crossed = block.at[rows_of(sig_peer(2), h_rows)]
            self.on = [
                describe(crossed, crossed, send_on, recv.at[k], {"sig": outer}) for k in (1, n_sig - 1)
            ] if relay else []

        def receive(self):
            for k in order:
                self.copies[k].wait_recv()
                if relay and k == 2:
                    when(sig == 1, self.on[0].start)
                    when(sig == n_sig - 2, self.on[1].start)

        def finish(self):
            for k in order:
                when(sends(k), self.copies[k].wait_send)
            if relay:
                when(sig == 1, self.on[0].wait_send)
                when(sig == n_sig - 2, self.on[1].wait_send)

    gather_h = Gather(fh_hbm, h_blk, send_h, recv_h, send_on.at[0])
    w_copies = [
        remote(fw_hbm, w_blk.at[rows_of(build, w_rows)], send_w.at[k], recv_w.at[k], {"build": build_peer(k)})
        for k in range(1, n_build)
    ]
    pending += w_copies
    for copy in local_copies:
        copy.wait()
    live = count[0, 0]
    down = lax.broadcasted_iota(jnp.int32, (slots, slots), 0)
    along = lax.broadcasted_iota(jnp.int32, (slots, slots), 1)
    for side in range(2):
        index_row = jnp.broadcast_to(index_ref[side], (slots, slots))
        index_col = jnp.sum(jnp.where(down == along, index_row, 0), axis=1, keepdims=True)
        index_col = jnp.broadcast_to(index_col, (slots, slots))
        same = (index_col == index_row) & (down < along) & (down < live)
        hit = (index_col == along) & (down < live)
        lines = [
            index_row[:1],
            jnp.max(jnp.where(same, down + 1, 0), axis=0, keepdims=True),
            jnp.max(jnp.where(hit, down + 1, 0), axis=0, keepdims=True),
        ]
        for i, line in enumerate(lines):
            link_ref[3 * side + i:3 * side + i + 1, 0:slots] = line
    link_copy = pltpu.make_async_copy(link_ref, meta, local_sem.at[4])
    link_copy.start()

    def link(line, place, most):
        return jnp.clip(meta[line, place], 0, most)

    h_blk[rows_of(sig, h_rows), :] = fh_ref[...]
    w_blk[rows_of(build, w_rows), :] = fw_ref[...]
    chain_h[0] = jnp.zeros(chain_h.shape[1:], f32)
    chain_w[0] = jnp.zeros(chain_w.shape[1:], f32)

    for copy in w_copies:
        copy.wait_recv()
    part = jnp.zeros((8, w_blk.shape[1]), f32)
    for r in range(row_tiles):
        block = w_blk[r * tile:(r + 1) * tile, :]
        w_tiles[r] = block
        w_turn[r] = block.T
        part += block.astype(f32).reshape(tile // 8, 8, -1).sum(axis=0)
    col_part[sig] = part
    ct_copies = [
        remote(col_part.at[sig], col_part.at[sig], send_ct.at[k], recv_ct.at[k], {"sig": sig_peer(k)})
        for k in range(1, n_sig)
    ]
    pending += ct_copies

    load.wait()
    link_copy.wait()
    gather_h.receive()
    for c in range(col_tiles):
        h_tiles[0, c] = h_blk[c * tile:(c + 1) * tile, :]

    def ratio_of(slot, w, h):
        product = lax.dot_general(w, h, (((1,), (1,)), ((), ())), preferred_element_type=f32)
        return (tiles[slot].astype(f32) / product).astype(bf16)

    def pass_h(step, carry):
        terms = []
        for g in range(GROUP):
            slot = step * GROUP + g
            row, col = link(0, slot, row_tiles - 1), link(3, slot, col_tiles - 1)
            ratio = ratio_of(slot, w_tiles[row], h_tiles[0, col])
            terms.append(jnp.dot(w_turn[row], ratio, preferred_element_type=f32))
        for g in range(GROUP):
            slot = step * GROUP + g
            chain_h[slot + 1] = chain_h[link(4, slot, slots)] + terms[g]
        return carry

    lax.fori_loop(0, slots // GROUP, pass_h, 0)
    for c in range(col_tiles):
        block = chain_h[link(5, c, slots)].T
        numer[c * tile:(c + 1) * tile, :] = block
        h_send[c * tile:(c + 1) * tile, :] = block.astype(bf16)
    nh_copies = {
        k: describe(h_send.at[rows_of(sig_peer(k), h_rows)], h_recv.at[sig], send_nh.at[k], recv_nh.at[k],
                    {"sig": sig_peer(k)})
        for k in order
    }
    hop = describe(h_send.at[rows_of(far, h_rows)], h_hop, send_on.at[2], recv_hop, {"sig": inner})
    if relay:
        when(is_end, hop.start)
    for k in order:
        when(is_end if relay and k == 2 else sends(k), nh_copies[k].start)
    if relay:
        @pl.when(jnp.logical_not(is_end))
        def _():
            hop.wait_recv()
            crossing = rows_of(sig_peer(2), h_rows)
            h_send[crossing, :] = (numer[crossing, :] + h_hop[...].astype(f32)).astype(bf16)
            nh_copies[2].start()
    for copy in ct_copies:
        copy.wait_recv()
    col_sum = col_part[0]
    for k in range(1, n_sig):
        col_sum += col_part[k]
    col_total = jnp.sum(col_sum, axis=0, keepdims=True)
    mine = rows_of(sig, h_rows)

    def add(k):
        nh_copies[k].wait_recv()
        numer[mine, :] += h_recv[sig_peer(n_sig - k)].astype(f32)

    for k in order[::-1]:
        arrives = None if not relay or k == 2 else sig != (n_sig - 1 if k == n_sig - 1 else 0)
        when(arrives, functools.partial(add, k))
    share = numer[mine, :]
    h_new = (fh_ref[...].astype(f32) * share / col_total).astype(bf16)
    h_next[mine, :] = h_new
    ext[HALO:HALO + h_rows, :] = h_new
    halo_copies = [
        remote(ext.at[h_rows:HALO + h_rows], ext.at[0:HALO], send_halo.at[0], recv_halo.at[0], at(above)),
        remote(ext.at[HALO:2 * HALO], ext.at[HALO + h_rows:2 * HALO + h_rows],
               send_halo.at[1], recv_halo.at[1], at(below)),
    ]
    gather_next = Gather(h_next.at[mine], h_next, send_h2, recv_h2, send_on.at[1])
    pending += halo_copies

    for copy in halo_copies:
        copy.wait_recv()
    signal = ext[...].astype(f32)
    length = signal.shape[0]
    position = index * h_rows - HALO + lax.broadcasted_iota(jnp.int32, signal.shape, 0)
    keep = (position >= 0) & (position < total * h_rows - 1)
    limit = jnp.where(keep, jnp.broadcast_to(tv_ref[...], signal.shape), 0.0)
    pull = TAU * (pltpu.roll(signal, length - 1, 0) - signal)

    def sweep(step, dual):
        around = pltpu.roll(dual, 1, 0) + pltpu.roll(dual, length - 1, 0)
        moved = pull + (1.0 - 2.0 * TAU) * dual + TAU * around
        return jnp.maximum(jnp.minimum(moved, limit), -limit)

    dual = lax.fori_loop(0, TV_STEPS, sweep, jnp.zeros_like(signal))
    smooth = signal - pltpu.roll(dual, 1, 0) + dual
    smooth_out[...] = smooth[HALO:HALO + h_rows, :]

    gather_next.receive()
    part = jnp.zeros((8, w_blk.shape[1]), f32)
    for c in range(col_tiles):
        block = h_next[c * tile:(c + 1) * tile, :]
        h_tiles[1, c] = block
        part += block.astype(f32).reshape(tile // 8, 8, -1).sum(axis=0)
    row_part[build] = part
    rt_copies = [
        remote(row_part.at[build], row_part.at[build], send_rt.at[k], recv_rt.at[k], {"build": build_peer(k)})
        for k in range(1, n_build)
    ]
    pending += rt_copies

    def pass_w(step, carry):
        terms = []
        for g in range(GROUP):
            slot = step * GROUP + g
            h = h_tiles[1, link(3, slot, col_tiles - 1)]
            ratio = ratio_of(slot, w_tiles[link(0, slot, row_tiles - 1)], h)
            terms.append(jnp.dot(ratio, h, preferred_element_type=f32))
        for g in range(GROUP):
            slot = step * GROUP + g
            chain_w[slot + 1] = chain_w[link(1, slot, slots)] + terms[g]
        return carry

    lax.fori_loop(0, slots // GROUP, pass_w, 0)
    for r in range(row_tiles):
        block = chain_w[link(2, r, slots)]
        numer[r * tile:(r + 1) * tile, :] = block
        w_send[r * tile:(r + 1) * tile, :] = block.astype(bf16)
    nw_copies = [
        remote(w_send.at[rows_of(build_peer(k), w_rows)], w_recv.at[build], send_nw.at[k], recv_nw.at[k],
               {"build": build_peer(k)})
        for k in range(1, n_build)
    ]
    pending += nw_copies
    for copy in rt_copies:
        copy.wait_recv()
    row_sum = row_part[0]
    for k in range(1, n_build):
        row_sum += row_part[k]
    row_total = jnp.sum(row_sum, axis=0, keepdims=True)
    share = numer[rows_of(build, w_rows), :]
    for k in range(1, n_build):
        nw_copies[k - 1].wait_recv()
        share += w_recv[build_peer(n_build - k)].astype(f32)
    w_out[...] = (fw_ref[...].astype(f32) * share / row_total).astype(bf16)
    for copy in pending:
        copy.wait_send()
    gather_h.finish()
    gather_next.finish()
    for k in order:
        when(sends(k), nh_copies[k].wait_send)
    if relay:
        when(is_end, hop.wait_send)


def local(n_sig, n_build, tiles, tile_rows, tile_cols, tile_count, factor_w, factor_h, tv_weight):
    tiles = tiles[0, 0]
    slots, tile = tiles.shape[:2]
    w_rows, rank = factor_w.shape
    h_rows = factor_h.shape[0]
    block_rows, block_cols = w_rows * n_build, h_rows * n_sig
    vmem, smem = pltpu.VMEM, pltpu.SMEM
    f32, bf16 = jnp.float32, jnp.bfloat16
    dma = pltpu.SemaphoreType.DMA
    in_vmem = pl.BlockSpec(memory_space=pltpu.VMEM)
    in_hbm = pl.BlockSpec(memory_space=pltpu.HBM)
    in_smem = pl.BlockSpec(memory_space=pltpu.SMEM)
    return pl.pallas_call(
        functools.partial(kernel, n_sig, n_build),
        out_shape=(
            jax.ShapeDtypeStruct((w_rows, rank), bf16),
            jax.ShapeDtypeStruct((h_rows, rank), f32),
        ),
        in_specs=[in_hbm, in_hbm, in_smem, in_hbm, in_hbm, in_hbm, in_vmem],
        out_specs=(in_vmem, in_vmem),
        scratch_shapes=[
            vmem((slots, tile, tile), bf16),
            vmem((block_rows, rank), bf16),
            vmem((block_rows // tile, rank, tile), bf16),
            vmem((block_cols, rank), bf16),
            vmem((block_cols, rank), bf16),
            vmem((block_rows // tile, tile, rank), bf16),
            vmem((2, block_cols // tile, tile, rank), bf16),
            vmem((slots + 1, rank, tile), f32),
            vmem((slots + 1, tile, rank), f32),
            vmem((max(block_rows, block_cols), rank), f32),
            vmem((block_cols, rank), bf16),
            vmem((n_sig, h_rows, rank), bf16),
            vmem((block_rows, rank), bf16),
            vmem((n_build, w_rows, rank), bf16),
            vmem((n_sig, 8, rank), f32),
            vmem((n_build, 8, rank), f32),
            vmem((h_rows + 2 * HALO, rank), bf16),
            vmem((w_rows, rank), bf16),
            vmem((h_rows, rank), bf16),
            vmem((2, 1, slots), jnp.int32),
            vmem((8, 128), jnp.int32),
            smem((8, 128), jnp.int32),
            vmem((h_rows, rank), bf16),
            dma((3,)), dma,
            dma, dma((5,)),
            dma((n_build,)), dma((n_build,)),
            dma((n_sig,)), dma((n_sig,)),
            dma((n_sig,)), dma((n_sig,)),
            dma((n_sig,)), dma((n_sig,)),
            dma((n_sig,)), dma((n_sig,)),
            dma((2,)), dma((2,)),
            dma((n_build,)), dma((n_build,)),
            dma((n_build,)), dma((n_build,)),
        ],
        compiler_params=pltpu.CompilerParams(
            collective_id=0, has_side_effects=True, vmem_limit_bytes=60 * 1024 * 1024
        ),
    )(tile_rows[0], tile_cols[0], tile_count, tiles, factor_w, factor_h, tv_weight[None, :])


def solution(mesh):
    return jax.shard_map(
        functools.partial(local, mesh.shape["sig"], mesh.shape["build"]),
        mesh=mesh,
        in_specs=(
            P(("groups", "sig"), "build", None, None, None),
            P(("groups", "sig"), "build", None),
            P(("groups", "sig"), "build", None),
            P(("groups", "sig"), "build"),
            P(("groups", "sig", "build"), None),
            P(("groups", "sig", "build"), None),
            P("groups"),
        ),
        out_specs=(P(("groups", "sig", "build"), None), P(("groups", "sig", "build"), None)),
        check_vma=False,
    )
```

```python
import functools

import jax
import jax.numpy as jnp
from jax import lax
from jax.experimental import pallas as pl
from jax.experimental.pallas import tpu as pltpu
from jax.sharding import PartitionSpec as P

TV_STEPS = 16
TAU = 0.25
HALO = 32
GROUP = 16
MESH = pl.DeviceIdType.MESH


def kernel(
    n_sig, n_build,
    rows_hbm, cols_hbm, count, tiles_hbm, fw_hbm, fh_hbm, tv_ref,
    w_out, smooth_out,
    tiles, w_blk, w_turn, h_blk, h_next, w_tiles, h_tiles, chain_h, chain_w, numer,
    h_send, h_recv, w_send, w_recv, col_part, row_part, ext,
    fw_ref, fh_ref, index_ref, link_ref, meta, h_hop, send_on, recv_hop, tile_sem, local_sem, send_w, recv_w, send_h, recv_h, send_ct, recv_ct, send_nh, recv_nh,
    send_h2, recv_h2, send_halo, recv_halo, send_rt, recv_rt, send_nw, recv_nw,
):
    f32, bf16 = jnp.float32, jnp.bfloat16
    sig = lax.axis_index("sig")
    build = lax.axis_index("build")
    slots, tile = tiles.shape[0], tiles.shape[1]
    w_rows, h_rows = fw_ref.shape[0], fh_ref.shape[0]
    row_tiles = w_blk.shape[0] // tile
    col_tiles = h_blk.shape[0] // tile

    load = pltpu.make_async_copy(tiles_hbm, tiles, tile_sem)
    load.start()
    local_copies = [
        pltpu.make_async_copy(src, dst, local_sem.at[i])
        for i, (src, dst) in enumerate([
            (fw_hbm, fw_ref), (fh_hbm, fh_ref),
            (rows_hbm, index_ref.at[0]), (cols_hbm, index_ref.at[1]),
        ])
    ]
    for copy in local_copies:
        copy.start()

    def sig_peer(k):
        return lax.rem(sig + k, n_sig)

    def build_peer(k):
        return lax.rem(build + k, n_build)

    total = n_sig * n_build
    index = sig * n_build + build
    above = lax.rem(index + 1, total)
    below = lax.rem(index + total - 1, total)

    def at(linear):
        return {"sig": lax.div(linear, n_build), "build": lax.rem(linear, n_build)}

    barrier = pltpu.get_barrier_semaphore()
    for k in range(1, n_sig):
        pl.semaphore_signal(barrier, inc=1, device_id={"sig": sig_peer(k)}, device_id_type=MESH)
    for k in range(1, n_build):
        pl.semaphore_signal(barrier, inc=1, device_id={"build": build_peer(k)}, device_id_type=MESH)
    pl.semaphore_signal(barrier, inc=1, device_id=at(above), device_id_type=MESH)
    pl.semaphore_signal(barrier, inc=1, device_id=at(below), device_id_type=MESH)
    pl.semaphore_wait(barrier, n_sig + n_build)

    def describe(src, dst, send, recv, device):
        return pltpu.make_async_remote_copy(
            src_ref=src, dst_ref=dst, send_sem=send, recv_sem=recv,
            device_id=device, device_id_type=MESH,
        )

    def remote(src, dst, send, recv, device):
        copy = describe(src, dst, send, recv, device)
        copy.start()
        return copy

    def rows_of(place, rows):
        return pl.ds(pl.multiple_of(place * rows, rows), rows)

    pending = []
    relay = n_sig == 4
    order = [2, 1, 3] if relay else list(range(1, n_sig))
    is_end = (sig == 0) | (sig == n_sig - 1)
    far = n_sig - 1 - sig
    inner = jnp.where(sig * 2 < n_sig, 1, n_sig - 2)
    outer = jnp.where(sig * 2 < n_sig, 0, n_sig - 1)

    def when(condition, action):
        if condition is None:
            action()
        else:
            pl.when(condition)(action)

    def sends(k):
        if not relay or k == 2:
            return None
        return sig != (0 if k == n_sig - 1 else n_sig - 1)

    class Gather:
        def __init__(self, src, block, send, recv, send_on):
            mine = block.at[rows_of(sig, h_rows)]
            self.copies = {
                k: describe(src, mine, send.at[k], recv.at[k], {"sig": sig_peer(k)}) for k in order
            }
            for k in order:
                when(sends(k), self.copies[k].start)
            crossed = block.at[rows_of(sig_peer(2), h_rows)]
            self.on = [
                describe(crossed, crossed, send_on, recv.at[k], {"sig": outer}) for k in (1, n_sig - 1)
            ] if relay else []

        def receive(self):
            for k in order:
                self.copies[k].wait_recv()
                if relay and k == 2:
                    when(sig == 1, self.on[0].start)
                    when(sig == n_sig - 2, self.on[1].start)

        def finish(self):
            for k in order:
                when(sends(k), self.copies[k].wait_send)
            if relay:
                when(sig == 1, self.on[0].wait_send)
                when(sig == n_sig - 2, self.on[1].wait_send)

    gather_h = Gather(fh_hbm, h_blk, send_h, recv_h, send_on.at[0])
    w_copies = [
        remote(fw_hbm, w_blk.at[rows_of(build, w_rows)], send_w.at[k], recv_w.at[k], {"build": build_peer(k)})
        for k in range(1, n_build)
    ]
    pending += w_copies
    for copy in local_copies:
        copy.wait()
    live = count[0, 0]
    down = lax.broadcasted_iota(jnp.int32, (slots, slots), 0)
    along = lax.broadcasted_iota(jnp.int32, (slots, slots), 1)
    for side in range(2):
        index_row = jnp.broadcast_to(index_ref[side], (slots, slots))
        index_col = jnp.sum(jnp.where(down == along, index_row, 0), axis=1, keepdims=True)
        index_col = jnp.broadcast_to(index_col, (slots, slots))
        same = (index_col == index_row) & (down < along) & (down < live)
        hit = (index_col == along) & (down < live)
        lines = [
            index_row[:1],
            jnp.max(jnp.where(same, down + 1, 0), axis=0, keepdims=True),
            jnp.max(jnp.where(hit, down + 1, 0), axis=0, keepdims=True),
        ]
        for i, line in enumerate(lines):
            link_ref[3 * side + i:3 * side + i + 1, 0:slots] = line
    link_copy = pltpu.make_async_copy(link_ref, meta, local_sem.at[4])
    link_copy.start()

    def link(line, place, most):
        return jnp.clip(meta[line, place], 0, most)

    h_blk[rows_of(sig, h_rows), :] = fh_ref[...]
    w_blk[rows_of(build, w_rows), :] = fw_ref[...]
    chain_h[0] = jnp.zeros(chain_h.shape[1:], f32)
    chain_w[0] = jnp.zeros(chain_w.shape[1:], f32)

    for copy in w_copies:
        copy.wait_recv()
    part = jnp.zeros((8, w_blk.shape[1]), f32)
    for r in range(row_tiles):
        block = w_blk[r * tile:(r + 1) * tile, :]
        w_tiles[r] = block
        w_turn[r] = block.T
        part += block.astype(f32).reshape(tile // 8, 8, -1).sum(axis=0)
    col_part[sig] = part
    ct_copies = [
        remote(col_part.at[sig], col_part.at[sig], send_ct.at[k], recv_ct.at[k], {"sig": sig_peer(k)})
        for k in range(1, n_sig)
    ]
    pending += ct_copies

    load.wait()
    link_copy.wait()
    gather_h.receive()
    for c in range(col_tiles):
        h_tiles[0, c] = h_blk[c * tile:(c + 1) * tile, :]

    def ratio_of(slot, w, h):
        product = lax.dot_general(w, h, (((1,), (1,)), ((), ())), preferred_element_type=f32)
        return (tiles[slot].astype(f32) / product).astype(bf16)

    def pass_h(step, carry):
        terms = []
        for g in range(GROUP):
            slot = step * GROUP + g
            row, col = link(0, slot, row_tiles - 1), link(3, slot, col_tiles - 1)
            ratio = ratio_of(slot, w_tiles[row], h_tiles[0, col])
            terms.append(jnp.dot(w_turn[row], ratio, preferred_element_type=f32))
        for g in range(GROUP):
            slot = step * GROUP + g
            chain_h[slot + 1] = chain_h[link(4, slot, slots)] + terms[g]
        return carry

    lax.fori_loop(0, slots // GROUP, pass_h, 0)
    for c in range(col_tiles):
        block = chain_h[link(5, c, slots)].T
        numer[c * tile:(c + 1) * tile, :] = block
        h_send[c * tile:(c + 1) * tile, :] = block.astype(bf16)
    nh_copies = {
        k: describe(h_send.at[rows_of(sig_peer(k), h_rows)], h_recv.at[sig], send_nh.at[k], recv_nh.at[k],
                    {"sig": sig_peer(k)})
        for k in order
    }
    hop = describe(h_send.at[rows_of(far, h_rows)], h_hop, send_on.at[2], recv_hop, {"sig": inner})
    if relay:
        when(is_end, hop.start)
    for k in order:
        when(is_end if relay and k == 2 else sends(k), nh_copies[k].start)
    if relay:
        @pl.when(jnp.logical_not(is_end))
        def _():
            hop.wait_recv()
            crossing = rows_of(sig_peer(2), h_rows)
            h_send[crossing, :] = (numer[crossing, :] + h_hop[...].astype(f32)).astype(bf16)
            nh_copies[2].start()
    for copy in ct_copies:
        copy.wait_recv()
    col_sum = col_part[0]
    for k in range(1, n_sig):
        col_sum += col_part[k]
    col_total = jnp.sum(col_sum, axis=0, keepdims=True)
    mine = rows_of(sig, h_rows)

    def add(k):
        nh_copies[k].wait_recv()
        numer[mine, :] += h_recv[sig_peer(n_sig - k)].astype(f32)

    for k in order[::-1]:
        arrives = None if not relay or k == 2 else sig != (n_sig - 1 if k == n_sig - 1 else 0)
        when(arrives, functools.partial(add, k))
    share = numer[mine, :]
    h_new = (fh_ref[...].astype(f32) * share / col_total).astype(bf16)
    h_next[mine, :] = h_new
    ext[HALO:HALO + h_rows, :] = h_new
    halo_copies = [
        remote(ext.at[h_rows:HALO + h_rows], ext.at[0:HALO], send_halo.at[0], recv_halo.at[0], at(above)),
        remote(ext.at[HALO:2 * HALO], ext.at[HALO + h_rows:2 * HALO + h_rows],
               send_halo.at[1], recv_halo.at[1], at(below)),
    ]
    gather_next = Gather(h_next.at[mine], h_next, send_h2, recv_h2, send_on.at[1])
    pending += halo_copies

    for copy in halo_copies:
        copy.wait_recv()
    signal = ext[...].astype(f32)
    length = signal.shape[0]
    position = index * h_rows - HALO + lax.broadcasted_iota(jnp.int32, signal.shape, 0)
    keep = (position >= 0) & (position < total * h_rows - 1)
    limit = jnp.where(keep, jnp.broadcast_to(tv_ref[...], signal.shape), 0.0)
    pull = TAU * (pltpu.roll(signal, length - 1, 0) - signal)

    def sweep(step, dual):
        around = pltpu.roll(dual, 1, 0) + pltpu.roll(dual, length - 1, 0)
        moved = pull + (1.0 - 2.0 * TAU) * dual + TAU * around
        return jnp.maximum(jnp.minimum(moved, limit), -limit)

    dual = lax.fori_loop(0, TV_STEPS, sweep, jnp.zeros_like(signal))
    smooth = signal - pltpu.roll(dual, 1, 0) + dual
    smooth_out[...] = smooth[HALO:HALO + h_rows, :]

    gather_next.receive()
    part = jnp.zeros((8, w_blk.shape[1]), f32)
    for c in range(col_tiles):
        block = h_next[c * tile:(c + 1) * tile, :]
        h_tiles[1, c] = block
        part += block.astype(f32).reshape(tile // 8, 8, -1).sum(axis=0)
    row_part[build] = part
    rt_copies = [
        remote(row_part.at[build], row_part.at[build], send_rt.at[k], recv_rt.at[k], {"build": build_peer(k)})
        for k in range(1, n_build)
    ]
    pending += rt_copies

    def pass_w(step, carry):
        terms = []
        for g in range(GROUP):
            slot = step * GROUP + g
            h = h_tiles[1, link(3, slot, col_tiles - 1)]
            ratio = ratio_of(slot, w_tiles[link(0, slot, row_tiles - 1)], h)
            terms.append(jnp.dot(ratio, h, preferred_element_type=f32))
        for g in range(GROUP):
            slot = step * GROUP + g
            chain_w[slot + 1] = chain_w[link(1, slot, slots)] + terms[g]
        return carry

    lax.fori_loop(0, slots // GROUP, pass_w, 0)
    per_shard = w_rows // tile
    nw_copies = []
    for k in list(range(1, n_build)) + [0]:
        owner = build_peer(k)
        for i in range(per_shard):
            block = chain_w[link(2, owner * per_shard + i, slots)]
            if k:
                w_send[rows_of(owner * per_shard + i, tile), :] = block.astype(bf16)
            else:
                numer[rows_of(owner * per_shard + i, tile), :] = block
        if k:
            nw_copies.append(
                remote(w_send.at[rows_of(owner, w_rows)], w_recv.at[build], send_nw.at[k], recv_nw.at[k],
                       {"build": owner})
            )
    pending += nw_copies
    for copy in rt_copies:
        copy.wait_recv()
    row_sum = row_part[0]
    for k in range(1, n_build):
        row_sum += row_part[k]
    row_total = jnp.sum(row_sum, axis=0, keepdims=True)
    share = numer[rows_of(build, w_rows), :]
    for k in range(1, n_build):
        nw_copies[k - 1].wait_recv()
        share += w_recv[build_peer(n_build - k)].astype(f32)
    w_out[...] = (fw_ref[...].astype(f32) * share / row_total).astype(bf16)
    for copy in pending:
        copy.wait_send()
    gather_h.finish()
    gather_next.finish()
    for k in order:
        when(sends(k), nh_copies[k].wait_send)
    if relay:
        when(is_end, hop.wait_send)


def local(n_sig, n_build, tiles, tile_rows, tile_cols, tile_count, factor_w, factor_h, tv_weight):
    tiles = tiles[0, 0]
    slots, tile = tiles.shape[:2]
    w_rows, rank = factor_w.shape
    h_rows = factor_h.shape[0]
    block_rows, block_cols = w_rows * n_build, h_rows * n_sig
    vmem, smem = pltpu.VMEM, pltpu.SMEM
    f32, bf16 = jnp.float32, jnp.bfloat16
    dma = pltpu.SemaphoreType.DMA
    in_vmem = pl.BlockSpec(memory_space=pltpu.VMEM)
    in_hbm = pl.BlockSpec(memory_space=pltpu.HBM)
    in_smem = pl.BlockSpec(memory_space=pltpu.SMEM)
    return pl.pallas_call(
        functools.partial(kernel, n_sig, n_build),
        out_shape=(
            jax.ShapeDtypeStruct((w_rows, rank), bf16),
            jax.ShapeDtypeStruct((h_rows, rank), f32),
        ),
        in_specs=[in_hbm, in_hbm, in_smem, in_hbm, in_hbm, in_hbm, in_vmem],
        out_specs=(in_vmem, in_vmem),
        scratch_shapes=[
            vmem((slots, tile, tile), bf16),
            vmem((block_rows, rank), bf16),
            vmem((block_rows // tile, rank, tile), bf16),
            vmem((block_cols, rank), bf16),
            vmem((block_cols, rank), bf16),
            vmem((block_rows // tile, tile, rank), bf16),
            vmem((2, block_cols // tile, tile, rank), bf16),
            vmem((slots + 1, rank, tile), f32),
            vmem((slots + 1, tile, rank), f32),
            vmem((max(block_rows, block_cols), rank), f32),
            vmem((block_cols, rank), bf16),
            vmem((n_sig, h_rows, rank), bf16),
            vmem((block_rows, rank), bf16),
            vmem((n_build, w_rows, rank), bf16),
            vmem((n_sig, 8, rank), f32),
            vmem((n_build, 8, rank), f32),
            vmem((h_rows + 2 * HALO, rank), bf16),
            vmem((w_rows, rank), bf16),
            vmem((h_rows, rank), bf16),
            vmem((2, 1, slots), jnp.int32),
            vmem((8, 128), jnp.int32),
            smem((8, 128), jnp.int32),
            vmem((h_rows, rank), bf16),
            dma((3,)), dma,
            dma, dma((5,)),
            dma((n_build,)), dma((n_build,)),
            dma((n_sig,)), dma((n_sig,)),
            dma((n_sig,)), dma((n_sig,)),
            dma((n_sig,)), dma((n_sig,)),
            dma((n_sig,)), dma((n_sig,)),
            dma((2,)), dma((2,)),
            dma((n_build,)), dma((n_build,)),
            dma((n_build,)), dma((n_build,)),
        ],
        compiler_params=pltpu.CompilerParams(
            collective_id=0, has_side_effects=True, vmem_limit_bytes=60 * 1024 * 1024
        ),
    )(tile_rows[0], tile_cols[0], tile_count, tiles, factor_w, factor_h, tv_weight[None, :])


def solution(mesh):
    return jax.shard_map(
        functools.partial(local, mesh.shape["sig"], mesh.shape["build"]),
        mesh=mesh,
        in_specs=(
            P(("groups", "sig"), "build", None, None, None),
            P(("groups", "sig"), "build", None),
            P(("groups", "sig"), "build", None),
            P(("groups", "sig"), "build"),
            P(("groups", "sig", "build"), None),
            P(("groups", "sig", "build"), None),
            P("groups"),
        ),
        out_specs=(P(("groups", "sig", "build"), None), P(("groups", "sig", "build"), None)),
        check_vma=False,
    )
```
